32 devices in a mesh: dp: 4 (over y, x), pipe: 4 (over z), tensor: 2 (over core).
Axes of the slice: x: 2, y: 2, z: 4, core: 2. Of those that a mesh axis runs over, the one named last changes fastest.
Arguments:
- tokens: bfloat16 [2048, 3072], P(('dp', 'tensor')), may hold values from -6 to 6
- destination: int32 [2048], P(('dp', 'tensor')), may hold values from 0 to 2047, as said below
- segments: int32 [16, 128], P('dp'), may hold values from 0 to 5, never falling along the last dimension, each value on 1 to 64 neighbouring positions
- query_weight: bfloat16 [4, 3072, 2048], P('pipe', None, 'tensor')
- key_value_weight: bfloat16 [4, 3072, 2048], P('pipe', None, 'tensor')
- out_weight: bfloat16 [4, 2048, 3072], P('pipe', 'tensor'), may hold values from -0.125 to 0.125
- gate_weight: bfloat16 [4, 3072, 8192], P('pipe', None, 'tensor'), may hold values from -0.109375 to 0.109375
- up_weight: bfloat16 [4, 3072, 8192], P('pipe', None, 'tensor'), may hold values from -0.109375 to 0.109375
- down_weight: bfloat16 [4, 8192, 3072], P('pipe', 'tensor'), may hold values from -0.0625 to 0.0625
- attention_gain: float32 [4, 3072], P('pipe'), may hold values from 0.1 to 1.9
- forward_gain: float32 [4, 3072], P('pipe'), may hold values from 0.1 to 1.9
Outputs:
- layers_out: float32 [2048, 3072], P(('dp', 'pipe', 'tensor'))
The draws below stay inside these ranges and needn't reach their ends.
Inputs may be any that keep to these rules, and one draw needn't show every extreme that they name: destination is a permutation of the 2048 rows. A row held at tensor index t goes to a place within its micro-batch in [t * 64, (t + 1) * 64). At most 128 rows of one device go to one dp index, and every device sends exactly 128 rows to some dp index.
All inputs are finite; a program needn't handle non-finite values.
Results may differ from the reference program's by a relative error of at most 0.04.
Values may be sent and summed in bfloat16 or wider, within the bound.
A program may use at most 192 MiB of HBM per device.

```python
import math
import jax
import jax.numpy as jnp
import numpy as np
from jax import lax

D = 3072
H = 16
KV = 8
HD = 128
FF = 8192
MB = 128
DOCS = 6
MICRO = 4
LAYERS = 4
TOKENS = 2048
ROWS = 256
CAP = 128
N_DP = 4
N_TENSOR = 2


def shared_keys(key):
    return jax.random.normal(key, (LAYERS, D, KV, 2, HD), jnp.float32) * D ** (-0.5)


def draw_key_value_weight(key, part):
    base = shared_keys(key)
    return base.reshape(LAYERS, D, 2 * KV * HD).astype(jnp.bfloat16)


def draw_query_weight(key, part):
    key = jax.random.fold_in(key, 7)
    own = jax.random.normal(key, (LAYERS, D, H, HD), jnp.float32) * D ** (-0.5)
    return own.reshape(LAYERS, D, H * HD).astype(jnp.bfloat16)


def draw_destination(key, part):
    key = jax.random.fold_in(key, 5)
    slab_rows = MB // N_TENSOR

    def one_slot(slot_key, tensor_index):
        cut_key, top_key, place_key, order_key = jax.random.split(slot_key, 4)
        cuts = jnp.sort(jax.random.randint(cut_key, (N_DP - 2,), 0, ROWS - CAP + 1))
        edges = jnp.concatenate([jnp.zeros((1,), jnp.int32), cuts.astype(jnp.int32), jnp.full((1,), ROWS - CAP, jnp.int32)])
        others = edges[1:] - edges[:-1]
        amounts = jnp.roll(jnp.concatenate([jnp.full((1,), CAP, jnp.int32), others]), jax.random.randint(top_key, (), 0, N_DP))
        ends = jnp.cumsum(amounts)
        order = jnp.arange(ROWS, dtype=jnp.int32)
        offset = jnp.sum((order[:, None] >= ends[None, :]).astype(jnp.int32), axis=1)
        places = jnp.stack([jax.random.permutation(jax.random.fold_in(place_key, group), ROWS) for group in range(N_DP)]).astype(jnp.int32)
        orders = jnp.stack([jax.random.permutation(jax.random.fold_in(order_key, group), ROWS) for group in range(N_DP)]).astype(jnp.int32)
        groups = jnp.arange(N_DP, dtype=jnp.int32)
        target = (groups[:, None] + offset[None, :]) % N_DP
        landing = places[target, order[None, :]]
        value = target * (MICRO * MB) + landing // slab_rows * MB + tensor_index * slab_rows + landing % slab_rows
        return jnp.zeros((N_DP, ROWS), jnp.int32).at[jnp.broadcast_to(groups[:, None], (N_DP, ROWS)), orders].set(value)
    table = jax.vmap(one_slot)(jax.random.split(key, N_TENSOR), jnp.arange(N_TENSOR, dtype=jnp.int32))
    return jnp.transpose(table, (1, 0, 2)).reshape(TOKENS)


def block_scale(key, dims, cuts, least, top_value):
    factor_of, own = 1.0, jax.random.fold_in(key, 6)
    for dim, blocks in cuts:
        heights = jnp.exp(jax.random.uniform(jax.random.fold_in(own, dim), (blocks,), jnp.float32, least / len(cuts), top_value / len(cuts)))
        factor_of = factor_of * jnp.repeat(heights, dims[dim] // blocks).reshape([-1 if axis == dim else 1 for axis in range(len(dims))])
    return factor_of


def split_up(count, total, most, lean):
    portions = [(1 << 20) // math.isqrt(standing ** lean) + 1 for standing in range(2, count + 1)]
    surplus, given = total - most - (count - 1), [1] * (count - 1)
    while surplus > 0:
        free = [i for i in range(count - 1) if given[i] < most]
        mass, budget = sum([portions[i] for i in free]), surplus
        for i in free:
            more = min(most - given[i], max(1, budget * portions[i] // mass), surplus)
            given[i] = given[i] + more
            surplus = surplus - more
    return np.array([most] + given)


def ragged_sizes(own_key, amount, total, most, skew):
    if amount == 2:
        one = jax.random.randint(own_key, (), max(1, total - most), min(most, total - 1) + 1)
        return jnp.stack([one, total - one])
    tallies = jnp.asarray(split_up(amount, total, most, skew), jnp.int32)
    twos = (amount - 1) // 2
    giver, receiver = tallies[1:1 + 2 * twos:2], tallies[2:2 + 2 * twos:2]
    room = jnp.minimum(giver - 1, most - receiver)
    shifted = jax.random.randint(jax.random.fold_in(own_key, 1), (twos,), 0, 1 << 20) % (room + 1)
    tallies = tallies.at[1:1 + 2 * twos:2].set(giver - shifted).at[2:2 + 2 * twos:2].set(receiver + shifted)
    return tallies[jax.random.permutation(jax.random.fold_in(own_key, 2), amount)]


def normal_values(stream_key, shape, deviation, most, pieces=(), kind=jnp.bfloat16):
    array = jax.random.normal(stream_key, shape, jnp.float32) * deviation
    if len(pieces) > 0:
        array = block_scale(stream_key, shape, pieces, -0.22, 0.18) * array
    return jnp.clip(array, min=-most, max=most).astype(kind)


def setup_inputs(seed: int = 0) -> dict:
    seeds = jax.random.split(jax.random.key(seed), 12)
    tokens = normal_values(seeds[0], (TOKENS, D), 1.0, 6.0, ((0, 8),))
    destination = draw_destination(jax.random.fold_in(seeds[11], 71), 0)
    segments = jax.vmap(lambda own: jnp.searchsorted(jnp.cumsum(ragged_sizes(own, DOCS, MB, MB // 2, 2)), jnp.arange(MB), side="right"))(jax.random.split(seeds[2], (N_DP * MICRO))).reshape((N_DP * MICRO, MB)).astype(jnp.int32)
    query_weight = draw_query_weight(jax.random.fold_in(seeds[11], 71), 0)
    key_value_weight = draw_key_value_weight(jax.random.fold_in(seeds[11], 71), 0)
    out_weight = normal_values(seeds[5], (LAYERS, H * HD, D), (H * HD) ** -0.5, 0.125, ((0, 4), (1, 2)))
    gate_weight = normal_values(seeds[6], (LAYERS, D, FF), D ** -0.5, 0.109375, ((0, 4), (2, 2)))
    up_weight = normal_values(seeds[7], (LAYERS, D, FF), D ** -0.5, 0.109375, ((0, 4), (2, 2)))
    down_weight = normal_values(seeds[8], (LAYERS, FF, D), FF ** -0.5, 0.0625, ((0, 4), (1, 2)))
    attention_gain = jnp.clip(1.0 + 0.18 * jax.random.normal(seeds[9], (LAYERS, D), jnp.float32), 0.1, 1.9)
    forward_gain = jnp.clip(1.0 + 0.18 * jax.random.normal(seeds[10], (LAYERS, D), jnp.float32), 0.1, 1.9)
    return {"tokens": tokens, "destination": destination, "segments": segments, "query_weight": query_weight, "key_value_weight": key_value_weight, "out_weight": out_weight, "gate_weight": gate_weight, "up_weight": up_weight, "down_weight": down_weight, "attention_gain": attention_gain, "forward_gain": forward_gain}


def doc_positions(doc_ids):
    order = jnp.arange(doc_ids.shape[0], dtype=jnp.int32)
    change = jnp.concatenate([jnp.ones((1,), dtype=bool), doc_ids[1:] != doc_ids[:-1]])
    starts = lax.cummax(jnp.where(change, order, jnp.zeros_like(order)), axis=0)
    return (order - starts).astype(jnp.float32)

def rotate(stack, places):
    half_width = stack.shape[-1] // 2
    frequency = 500000.0 ** (-(jnp.arange(half_width, dtype=jnp.float32) * 2.0 / stack.shape[-1]))
    angles = places[:, None] * frequency[None, :]
    cosine = jnp.cos(angles)[:, None, :]
    sine_part = jnp.sin(angles)[:, None, :]
    front_half = stack[..., :half_width]
    back_half = stack[..., half_width:]
    return jnp.concatenate([front_half * cosine - back_half * sine_part, back_half * cosine + front_half * sine_part], axis=-1)

def normalize(rows_in, gain):
    values = rows_in.astype(jnp.float32)
    meansq = lax.optimization_barrier(jnp.mean(values * values, axis=-1, keepdims=True))
    return (values * lax.rsqrt(meansq + 1e-05) * gain.astype(jnp.float32)).astype(jnp.bfloat16)

def visible(doc_ids):
    order = jnp.arange(doc_ids.shape[0], dtype=jnp.int32)
    return jnp.logical_and(doc_ids[:, None] == doc_ids[None, :], order[None, :] <= order[:, None])

def attend(queries, key_heads, value_heads, doc_ids):
    rows, heads_here, head_width = queries.shape
    shared_heads = key_heads.shape[1]
    grouped_queries = queries.reshape(rows, shared_heads, heads_here // shared_heads, head_width).astype(jnp.float32)
    scores = jnp.einsum('qagd,kad->agqk', grouped_queries, key_heads.astype(jnp.float32), precision=lax.Precision.HIGHEST) * head_width ** (-0.5)
    scores = jnp.where(visible(doc_ids), scores, jnp.float32(-1e+30))
    row_max = lax.optimization_barrier(jnp.max(scores, axis=-1, keepdims=True))
    spread = jnp.exp(scores - row_max)
    weights = (spread / lax.optimization_barrier(jnp.sum(spread, axis=-1, keepdims=True))).astype(jnp.bfloat16)
    mixed = jnp.einsum('agqk,kad->qagd', weights.astype(jnp.float32), value_heads.astype(jnp.float32))
    return mixed.astype(jnp.bfloat16).reshape(rows, heads_here * head_width)

def grouped_sum(left, right, group_count):
    rows, inner = left.shape
    left_groups = left.reshape(rows, group_count, inner // group_count).astype(jnp.float32)
    right_groups = right.reshape(group_count, inner // group_count, right.shape[1]).astype(jnp.float32)
    parts = jnp.einsum('rgk,gkd->grd', left_groups, right_groups)
    rounded = lax.optimization_barrier(parts.astype(jnp.bfloat16))
    return lax.optimization_barrier(jnp.sum(rounded.astype(jnp.float32), axis=0))

def layer_step(rows_now, doc_ids, query_local, pair_local, out_local, gate_local, up_local, down_local, gain_attention, gain_forward):
    places = doc_positions(doc_ids)
    normed = normalize(rows_now, gain_attention)
    query_proj = jnp.dot(normed, query_local, preferred_element_type=jnp.float32)
    queries = rotate(query_proj.reshape(MB, H, HD), places)
    pairs = jnp.dot(normed, pair_local, preferred_element_type=jnp.float32).reshape(MB, KV, 2, HD)
    key_heads = rotate(pairs[:, :, 0], places)
    value_heads = pairs[:, :, 1].astype(jnp.bfloat16)
    mixed = attend(queries, key_heads, value_heads, doc_ids)
    attn_total = grouped_sum(mixed, out_local, N_TENSOR)
    halfway = rows_now + attn_total
    normed_two = normalize(halfway, gain_forward)
    gate = jnp.dot(normed_two, gate_local, preferred_element_type=jnp.float32)
    upward = jnp.dot(normed_two, up_local, preferred_element_type=jnp.float32)
    hidden = (jax.nn.silu(gate) * upward).astype(jnp.bfloat16)
    forward_total = grouped_sum(hidden, down_local, N_TENSOR)
    return halfway + forward_total

def reference(tokens, destination, segments, query_weight, key_value_weight, out_weight, gate_weight, up_weight, down_weight, attention_gain, forward_gain):
    regrouped = jnp.zeros_like(tokens).at[destination].set(tokens)
    batches = regrouped.reshape(N_DP * MICRO, MB, D)

    def run(item):
        rows_in, doc_ids = item
        rows_now = rows_in.astype(jnp.float32)
        for layer in range(LAYERS):
            rows_now = layer_step(rows_now, doc_ids, query_weight[layer], key_value_weight[layer], out_weight[layer], gate_weight[layer], up_weight[layer], down_weight[layer], attention_gain[layer], forward_gain[layer])
        return rows_now
    return lax.map(run, (batches, segments)).reshape(TOKENS, D)
```

```python
import jax
import jax.numpy as jnp
from jax import lax
from jax.experimental import pallas as pl
from jax.experimental.pallas import tpu as pltpu
from jax.sharding import PartitionSpec as P

KV = 8
HD = 128
SLOTS = 8
CHUNK = 256


def swapped(value, axis, apart):
    mask = 2**apart
    pairs = [(source, source ^ mask) for source in range(lax.axis_size(axis))]
    return lax.ppermute(value, axis, pairs)


def shifted(array, axis, by):
    peers = lax.axis_size(axis)
    pairs = [(i, i + by) for i in range(peers) if 0 <= i + by < peers]
    return lax.ppermute(array, axis, pairs)


def broadcast(block, axis, source):
    block = jnp.where(lax.axis_index(axis) == source, block, jnp.zeros_like(block))
    return lax.psum(block, axis)


def doc_positions(doc_ids):
    order = jnp.arange(doc_ids.shape[0], dtype=jnp.int32)
    change = jnp.concatenate([jnp.ones((1,), dtype=bool), doc_ids[1:] != doc_ids[:-1]])
    starts = lax.cummax(jnp.where(change, order, jnp.zeros_like(order)), axis=0)
    return (order - starts).astype(jnp.float32)


def rotate(stack, places):
    half_width = stack.shape[-1] // 2
    frequency = 500000.0 ** (-(jnp.arange(half_width, dtype=jnp.float32) * 2.0 / stack.shape[-1]))
    angles = places[:, None] * frequency[None, :]
    cosine = jnp.cos(angles)[:, None, :]
    sine_part = jnp.sin(angles)[:, None, :]
    front_half = stack[..., :half_width]
    back_half = stack[..., half_width:]
    return jnp.concatenate(
        [front_half * cosine - back_half * sine_part, back_half * cosine + front_half * sine_part],
        axis=-1,
    )


def normalize(rows_in, gain):
    meansq = jnp.mean(rows_in * rows_in, axis=-1, keepdims=True)
    return (rows_in * lax.rsqrt(meansq + 1e-05) * gain).astype(jnp.bfloat16)


def visible(doc_ids):
    order = jnp.arange(doc_ids.shape[0], dtype=jnp.int32)
    return jnp.logical_and(doc_ids[:, None] == doc_ids[None, :], order[None, :] <= order[:, None])


def attend(queries, key_heads, value_heads, doc_ids):
    rows, heads_here, head_width = queries.shape
    shared_heads = key_heads.shape[1]
    grouped_queries = queries.reshape(rows, shared_heads, heads_here // shared_heads, head_width)
    scores = jnp.einsum(
        "qagd,kad->agqk",
        grouped_queries,
        key_heads,
        precision=lax.Precision.HIGHEST,
        preferred_element_type=jnp.float32,
    ) * head_width ** (-0.5)
    scores = jnp.where(visible(doc_ids), scores, jnp.float32(-1e30))
    row_max = jnp.max(scores, axis=-1, keepdims=True)
    spread = jnp.exp(scores - row_max)
    weights = (spread / jnp.sum(spread, axis=-1, keepdims=True)).astype(jnp.bfloat16)
    mixed = jnp.einsum("agqk,kad->qagd", weights, value_heads, preferred_element_type=jnp.float32)
    return mixed.astype(jnp.bfloat16).reshape(rows, heads_here * head_width)


def expand(rows_in, gate_local, up_local):
    gate = jnp.dot(rows_in, gate_local, preferred_element_type=jnp.float32)
    upward = jnp.dot(rows_in, up_local, preferred_element_type=jnp.float32)
    return (jax.nn.silu(gate) * upward).astype(jnp.bfloat16)


def split_pairs(pairs, places, tensor_count):
    rows = pairs.shape[0]
    if tensor_count > KV:
        parity = lax.axis_index("tensor") % 2
        turned = rotate(pairs.reshape(rows, 1, HD), places).reshape(rows, HD)
        mine = jnp.where(parity == 0, turned, pairs)
        partner = swapped(mine.astype(jnp.bfloat16), "tensor", 0).astype(mine.dtype)
        key_heads = jnp.where(parity == 0, mine, partner).reshape(rows, 1, HD)
        value_heads = (
            jnp.where(parity == 0, partner, mine).astype(jnp.bfloat16).reshape(rows, 1, HD)
        )
    else:
        grouped = pairs.reshape(rows, -1, 2, HD)
        key_heads = rotate(grouped[:, :, 0], places)
        value_heads = grouped[:, :, 1].astype(jnp.bfloat16)
    return (key_heads, value_heads)


def run_layer(current, doc_ids, layer_weights):
    (
        query_local,
        pair_local,
        out_local,
        gate_local,
        up_local,
        down_local,
        gain_attention,
        gain_forward,
    ) = layer_weights
    tensor_count = lax.axis_size("tensor")
    micro_rows = doc_ids.shape[0]
    query_cols = query_local.shape[1]
    places = doc_positions(doc_ids)
    piece = lax.all_gather(normalize(current, gain_attention), "tensor", axis=0, tiled=True)
    projected = jnp.concatenate(
        [
            jnp.dot(piece, query_local, preferred_element_type=jnp.float32),
            jnp.dot(piece, pair_local, preferred_element_type=jnp.float32),
        ],
        axis=1,
    )
    heads_here = query_cols // HD
    queries = rotate(projected[:, :query_cols].reshape(micro_rows, heads_here, HD), places)
    key_heads, value_heads = split_pairs(projected[:, query_cols:], places, tensor_count)
    mixed = attend(queries, key_heads, value_heads, doc_ids)
    total = lax.psum_scatter(
        jnp.dot(mixed, out_local, preferred_element_type=jnp.float32).astype(jnp.bfloat16),
        "tensor",
        scatter_dimension=0,
        tiled=True,
    ).astype(jnp.float32)
    halfway = current + total
    hidden = expand(
        lax.all_gather(normalize(halfway, gain_forward), "tensor", axis=0, tiled=True),
        gate_local,
        up_local,
    )
    forward = lax.psum_scatter(
        jnp.dot(hidden, down_local, preferred_element_type=jnp.float32).astype(jnp.bfloat16),
        "tensor",
        scatter_dimension=0,
        tiled=True,
    ).astype(jnp.float32)
    return halfway + forward


def pass_on(result):
    return shifted(result.astype(jnp.bfloat16), "pipe", 1).astype(result.dtype)


def section_kernel(
    x_ref,
    cos_ref,
    sin_ref,
    bias_ref,
    gain_one_ref,
    gain_two_ref,
    query_ref,
    pair_ref,
    out_ref,
    gate_ref,
    up_ref,
    down_ref,
    result_ref,
    left_buf,
    right_buf,
    tail_buf,
    full_one,
    full_two,
    total,
    outgoing,
    incoming,
    halfway,
    weight_sem,
    send_sem,
    recv_sem,
):
    mine = lax.axis_index("tensor")
    peer = 1 - mine
    rows = x_ref.shape[0]
    heads_steps = query_ref.shape[1] // CHUNK
    hidden_steps = gate_ref.shape[1] // CHUNK
    my_rows = pl.ds(pl.multiple_of(mine * rows, rows), rows)
    peer_rows = pl.ds(pl.multiple_of(peer * rows, rows), rows)

    def weight_copies(left, right, tail, index, slot):
        cols = pl.ds(pl.multiple_of(index * CHUNK, CHUNK), CHUNK)
        return (
            pltpu.make_async_copy(left.at[:, cols], left_buf.at[slot], weight_sem.at[0, slot]),
            pltpu.make_async_copy(right.at[:, cols], right_buf.at[slot], weight_sem.at[1, slot]),
            pltpu.make_async_copy(tail.at[cols, :], tail_buf.at[slot], weight_sem.at[2, slot]),
        )

    def attention_copies(index, slot):
        return weight_copies(query_ref, pair_ref, out_ref, index, slot)

    def hidden_copies(index, slot):
        return weight_copies(gate_ref, up_ref, down_ref, index, slot)

    for step in range(SLOTS):
        if step < heads_steps:
            copies = attention_copies(step, step)
        else:
            copies = hidden_copies(step - heads_steps, step)
        for copy in copies:
            copy.start()

    barrier = pltpu.get_barrier_semaphore()
    pl.semaphore_signal(
        barrier, inc=1, device_id={"tensor": peer}, device_id_type=pl.DeviceIdType.MESH
    )
    pl.semaphore_wait(barrier, 1)

    def send(source, target, index):
        return pltpu.make_async_remote_copy(
            src_ref=source,
            dst_ref=target,
            send_sem=send_sem.at[index],
            recv_sem=recv_sem.at[index],
            device_id={"tensor": peer},
            device_id_type=pl.DeviceIdType.MESH,
        )

    def share(values, gain, full, index):
        meansq = jnp.mean(values * values, axis=-1, keepdims=True)
        full[my_rows, :] = (values * lax.rsqrt(meansq + 1e-05) * gain).astype(jnp.bfloat16)
        copy = send(full.at[my_rows, :], full.at[my_rows, :], index)
        copy.start()
        copy.wait()

    def reduce(index):
        outgoing[index] = total[peer_rows, :].astype(jnp.bfloat16)
        copy = send(outgoing.at[index], incoming.at[index], 2 + index)
        copy.start()
        copy.wait()
        own = total[my_rows, :].astype(jnp.bfloat16).astype(jnp.float32)
        return own + incoming[index].astype(jnp.float32)

    def rotated(values):
        return values * cos_ref[...] + pltpu.roll(values, HD // 2, 1) * sin_ref[...]

    share(x_ref[...].astype(jnp.float32), gain_one_ref[...], full_one, 0)
    total[...] = jnp.zeros_like(total)

    def attention_step(step, carry):
        slot = lax.rem(step, SLOTS)
        for copy in attention_copies(step, slot):
            copy.wait()
        normed = full_one[...]
        queries = jnp.dot(normed, left_buf[slot], preferred_element_type=jnp.float32)
        pair = jnp.dot(normed, right_buf[slot], preferred_element_type=jnp.float32)
        keys = rotated(pair[:, :HD]).astype(jnp.bfloat16)
        values = pair[:, HD:].astype(jnp.bfloat16)
        mixed = []
        for head in range(2):
            query = rotated(queries[:, head * HD : (head + 1) * HD]).astype(jnp.bfloat16)
            scores = lax.dot_general(
                query, keys, (((1,), (1,)), ((), ())), preferred_element_type=jnp.float32
            )
            scores = scores * HD ** (-0.5) + bias_ref[...]
            spread = jnp.exp(scores - jnp.max(scores, axis=-1, keepdims=True))
            weights = spread / jnp.sum(spread, axis=-1, keepdims=True)
            mixed.append(
                jnp.dot(weights.astype(jnp.bfloat16), values, preferred_element_type=jnp.float32)
            )
        both = jnp.concatenate(mixed, axis=1).astype(jnp.bfloat16)
        total[...] += jnp.dot(both, tail_buf[slot], preferred_element_type=jnp.float32)
        for copy in hidden_copies(step + SLOTS - heads_steps, slot):
            copy.start()
        return carry

    lax.fori_loop(0, heads_steps, attention_step, 0)

    halfway[...] = x_ref[...].astype(jnp.float32) + reduce(0)
    share(halfway[...], gain_two_ref[...], full_two, 1)
    total[...] = jnp.zeros_like(total)

    def hidden_step(step, carry):
        slot = lax.rem(step + heads_steps, SLOTS)
        for copy in hidden_copies(step, slot):
            copy.wait()
        normed = full_two[...]
        gate = jnp.dot(normed, left_buf[slot], preferred_element_type=jnp.float32)
        upward = jnp.dot(normed, right_buf[slot], preferred_element_type=jnp.float32)
        hidden = (gate / (1.0 + jnp.exp(-gate)) * upward).astype(jnp.bfloat16)
        total[...] += jnp.dot(hidden, tail_buf[slot], preferred_element_type=jnp.float32)

        @pl.when(step + SLOTS < hidden_steps)
        def _():
            for copy in hidden_copies(step + SLOTS, slot):
                copy.start()

        return carry

    lax.fori_loop(0, hidden_steps, hidden_step, 0)
    result_ref[...] = (halfway[...] + reduce(1)).astype(jnp.bfloat16)


def run_section(current, cosine, sine, bias, layer_weights):
    (
        query_local,
        pair_local,
        out_local,
        gate_local,
        up_local,
        down_local,
        gain_attention,
        gain_forward,
    ) = layer_weights
    rows, width = current.shape
    resident = pl.BlockSpec(memory_space=pltpu.VMEM)
    streamed = pl.BlockSpec(memory_space=pl.ANY)
    return pl.pallas_call(
        section_kernel,
        out_shape=jax.ShapeDtypeStruct((rows, width), jnp.bfloat16),
        in_specs=[resident] * 6 + [streamed] * 6,
        out_specs=resident,
        scratch_shapes=[
            pltpu.VMEM((SLOTS, width, CHUNK), jnp.bfloat16),
            pltpu.VMEM((SLOTS, width, CHUNK), jnp.bfloat16),
            pltpu.VMEM((SLOTS, CHUNK, width), jnp.bfloat16),
            pltpu.VMEM((2 * rows, width), jnp.bfloat16),
            pltpu.VMEM((2 * rows, width), jnp.bfloat16),
            pltpu.VMEM((2 * rows, width), jnp.float32),
            pltpu.VMEM((2, rows, width), jnp.bfloat16),
            pltpu.VMEM((2, rows, width), jnp.bfloat16),
            pltpu.VMEM((rows, width), jnp.float32),
            pltpu.SemaphoreType.DMA((3, SLOTS)),
            pltpu.SemaphoreType.DMA((4,)),
            pltpu.SemaphoreType.DMA((4,)),
        ],
        compiler_params=pltpu.CompilerParams(
            collective_id=0, has_side_effects=True, vmem_limit_bytes=60 * 2**20
        ),
        cost_estimate=pl.CostEstimate(
            flops=2 * 2 * rows * 5 * CHUNK * width * 12,
            bytes_accessed=5 * CHUNK * width * 24,
            transcendentals=0,
        ),
    )(
        current,
        cosine,
        sine,
        bias,
        gain_attention[None, :],
        gain_forward[None, :],
        query_local,
        pair_local,
        out_local,
        gate_local,
        up_local,
        down_local,
    )


def regroup(tokens, destination, micro_count, micro_rows):
    group_count = lax.axis_size("dp")
    slab_rows = micro_rows // lax.axis_size("tensor")
    held_rows, width = tokens.shape
    capacity = held_rows // 2
    group_span = micro_count * micro_rows
    everywhere = lax.all_gather(destination, "dp", axis=0)
    groups = jnp.arange(group_count, dtype=jnp.int32)
    target = everywhere // group_span
    within = everywhere % group_span
    landing = within // micro_rows * slab_rows + within % slab_rows
    member = (target[:, None, :] == groups[None, :, None]).astype(jnp.int32)
    before = jnp.sum((jnp.cumsum(member, axis=2) - member) * member, axis=1)
    slots = jnp.arange(group_count * capacity, dtype=jnp.int32)
    me = lax.axis_index("dp")
    own = lax.dynamic_index_in_dim(target * capacity + before, me, 0, keepdims=False)
    pack = (slots[:, None] == own[None, :]).astype(jnp.bfloat16)
    send_rows = jnp.dot(pack, tokens, preferred_element_type=jnp.float32).astype(jnp.bfloat16)
    got_rows = lax.all_to_all(
        send_rows.reshape(group_count, capacity, width),
        "dp",
        split_axis=0,
        concat_axis=0,
        tiled=True,
    )
    arrives = (groups[:, None] * capacity + before).reshape(-1)
    lands = jnp.where(target == me, landing, -1).reshape(-1)
    order = jnp.arange(held_rows, dtype=jnp.int32)
    unpack = jnp.dot(
        (order[:, None] == lands[None, :]).astype(jnp.bfloat16),
        (arrives[:, None] == slots[None, :]).astype(jnp.bfloat16),
        preferred_element_type=jnp.float32,
    ).astype(jnp.bfloat16)
    return jnp.dot(
        unpack, got_rows.reshape(-1, width), preferred_element_type=jnp.float32
    ).astype(jnp.bfloat16)


def section_tables(doc_ids):
    group, micro_rows = doc_ids.shape
    tensor_count = lax.axis_size("tensor")

    def laid(table):
        by_slab = table.reshape(group, tensor_count, micro_rows // tensor_count)
        return jnp.swapaxes(by_slab, 0, 1).reshape(-1)

    places = laid(jax.vmap(doc_positions)(doc_ids))
    order = laid(jnp.broadcast_to(jnp.arange(micro_rows, dtype=jnp.int32), doc_ids.shape))
    batch = laid(jnp.broadcast_to(jnp.arange(group, dtype=jnp.int32)[:, None], doc_ids.shape))
    docs = laid(doc_ids)
    shown = (
        (docs[:, None] == docs[None, :])
        & (batch[:, None] == batch[None, :])
        & (order[None, :] <= order[:, None])
    )
    bias = jnp.where(shown, jnp.float32(0), jnp.float32(-1e30))
    frequency = 500000.0 ** (-(jnp.arange(HD // 2, dtype=jnp.float32) * 2.0 / HD))
    angles = places[:, None] * frequency[None, :]
    cosine, sine = jnp.cos(angles), jnp.sin(angles)
    return (
        jnp.concatenate([cosine, cosine], axis=1),
        jnp.concatenate([-sine, sine], axis=1),
        bias,
    )


def paired_shards(tokens, destination, segments, layer_weights):
    pipe_count = lax.axis_size("pipe")
    micro_count, micro_rows = segments.shape
    slab_rows = micro_rows // lax.axis_size("tensor")
    width = tokens.shape[1]
    group = 2
    group_rows = group * slab_rows
    rounds = micro_count // group
    regrouped = regroup(tokens, destination, micro_count, micro_rows)
    phase_index = lax.axis_index("pipe")
    tables = [section_tables(segments[r * group : (r + 1) * group]) for r in range(rounds)]
    carried = None
    mine = jnp.zeros((slab_rows, width), jnp.bfloat16)
    for moment in range(rounds + pipe_count - 1):
        feed = min(moment, rounds - 1)
        current = regrouped[feed * group_rows : (feed + 1) * group_rows]
        if carried is not None:
            current = jnp.where(phase_index == 0, current, carried)
        round_index = jnp.clip(moment - phase_index, 0, rounds - 1)
        cosine, sine, bias = (
            lax.select_n(round_index, *[table[i] for table in tables]) for i in range(3)
        )
        result = run_section(current, cosine, sine, bias, layer_weights)
        done = moment - (pipe_count - 1)
        if done >= 0:
            for inner in range(group):
                piece = result[inner * slab_rows : (inner + 1) * slab_rows]
                home = done * group + inner
                if home != pipe_count - 1:
                    piece = lax.ppermute(piece, "pipe", [(pipe_count - 1, home)])
                mine = jnp.where(phase_index == home, piece, mine)
        if moment < rounds + pipe_count - 2:
            carried = shifted(result, "pipe", 1)
    return mine.astype(jnp.float32)


def shards(
    tokens,
    destination,
    segments,
    query_weight,
    key_value_weight,
    out_weight,
    gate_weight,
    up_weight,
    down_weight,
    attention_gain,
    forward_gain,
):
    if lax.axis_size("tensor") == 2:
        layer_weights = (
            query_weight[0],
            key_value_weight[0],
            out_weight[0],
            gate_weight[0],
            up_weight[0],
            down_weight[0],
            attention_gain[0],
            forward_gain[0],
        )
        return paired_shards(tokens, destination, segments, layer_weights)
    group_count = lax.axis_size("dp")
    tensor_count = lax.axis_size("tensor")
    pipe_count = lax.axis_size("pipe")
    micro_count, micro_rows = segments.shape
    slab_rows = micro_rows // tensor_count
    held_rows, width = tokens.shape
    capacity = held_rows // 2
    group_span = micro_count * micro_rows
    target = destination // group_span
    within = destination % group_span
    landing = within // micro_rows * slab_rows + within % slab_rows
    member = (target[:, None] == jnp.arange(group_count, dtype=jnp.int32)[None, :]).astype(
        jnp.int32
    )
    before = jnp.sum((jnp.cumsum(member, axis=0) - member) * member, axis=1)
    slot_index = target * capacity + before
    send_rows = jnp.zeros((group_count * capacity, width), jnp.bfloat16).at[slot_index].set(tokens)
    send_places = (
        jnp.full((group_count * capacity,), held_rows, jnp.int32).at[slot_index].set(landing)
    )
    got_rows, got_places = (
        lax.all_to_all(
            send_rows.reshape(group_count, capacity, width),
            "dp",
            split_axis=0,
            concat_axis=0,
            tiled=True,
        ),
        lax.all_to_all(
            send_places.reshape(group_count, capacity),
            "dp",
            split_axis=0,
            concat_axis=0,
            tiled=True,
        ),
    )
    regrouped = (
        jnp.zeros((held_rows, width), jnp.bfloat16)
        .at[got_places.reshape(-1)]
        .set(got_rows.reshape(-1, width), mode="drop")
    )
    micro_batches = regrouped.reshape(micro_count, slab_rows, width)
    layer_weights = (
        query_weight[0],
        key_value_weight[0],
        out_weight[0],
        gate_weight[0],
        up_weight[0],
        down_weight[0],
        attention_gain[0],
        forward_gain[0],
    )
    phase_index = lax.axis_index("pipe")
    carried = jnp.zeros((slab_rows, width), jnp.float32)
    finished = []
    for moment in range(micro_count + pipe_count - 1):
        feed_rows = micro_batches[min(moment, micro_count - 1)].astype(jnp.float32)
        current = jnp.where(
            jnp.logical_and(phase_index == 0, moment < micro_count), feed_rows, carried
        )
        micro_index = jnp.clip(moment - phase_index, 0, micro_count - 1)
        doc_ids = lax.dynamic_index_in_dim(segments, micro_index, 0, keepdims=False)
        result = run_layer(current, doc_ids, layer_weights)
        if moment >= pipe_count - 1:
            finished.append(result)
        if moment < micro_count + pipe_count - 2:
            carried = pass_on(result)
    everyone = broadcast(jnp.stack(finished).astype(jnp.bfloat16), "pipe", pipe_count - 1).astype(
        jnp.float32
    )
    return lax.dynamic_index_in_dim(everyone, phase_index, 0, keepdims=False)


def solution(mesh):
    placed = (
        P(("dp", "tensor"), None),
        P(("dp", "tensor")),
        P("dp", None),
        P("pipe", None, "tensor"),
        P("pipe", None, "tensor"),
        P("pipe", "tensor", None),
        P("pipe", None, "tensor"),
        P("pipe", None, "tensor"),
        P("pipe", "tensor", None),
        P("pipe", None),
        P("pipe", None),
    )
    return jax.shard_map(
        shards,
        mesh=mesh,
        in_specs=placed,
        out_specs=P(("dp", "pipe", "tensor"), None),
        check_vma=False,
    )
```

```python
import functools

import jax
import jax.numpy as jnp
from jax import lax
from jax.experimental import pallas as pl
from jax.experimental.pallas import tpu as pltpu
from jax.sharding import PartitionSpec as P

KV = 8
HD = 128
SLOTS = 4
CHUNK = 512
PIECES = 4


def swapped(value, axis, apart):
    mask = 2**apart
    pairs = [(source, source ^ mask) for source in range(lax.axis_size(axis))]
    return lax.ppermute(value, axis, pairs)


def shifted(array, axis, by):
    peers = lax.axis_size(axis)
    pairs = [(i, i + by) for i in range(peers) if 0 <= i + by < peers]
    return lax.ppermute(array, axis, pairs)


def broadcast(block, axis, source):
    block = jnp.where(lax.axis_index(axis) == source, block, jnp.zeros_like(block))
    return lax.psum(block, axis)


def doc_positions(doc_ids):
    order = jnp.arange(doc_ids.shape[0], dtype=jnp.int32)
    change = jnp.concatenate([jnp.ones((1,), dtype=bool), doc_ids[1:] != doc_ids[:-1]])
    starts = lax.cummax(jnp.where(change, order, jnp.zeros_like(order)), axis=0)
    return (order - starts).astype(jnp.float32)


def rotate(stack, places):
    half_width = stack.shape[-1] // 2
    frequency = 500000.0 ** (-(jnp.arange(half_width, dtype=jnp.float32) * 2.0 / stack.shape[-1]))
    angles = places[:, None] * frequency[None, :]
    cosine = jnp.cos(angles)[:, None, :]
    sine_part = jnp.sin(angles)[:, None, :]
    front_half = stack[..., :half_width]
    back_half = stack[..., half_width:]
    return jnp.concatenate(
        [front_half * cosine - back_half * sine_part, back_half * cosine + front_half * sine_part],
        axis=-1,
    )


def normalize(rows_in, gain):
    meansq = jnp.mean(rows_in * rows_in, axis=-1, keepdims=True)
    return (rows_in * lax.rsqrt(meansq + 1e-05) * gain).astype(jnp.bfloat16)


def visible(doc_ids):
    order = jnp.arange(doc_ids.shape[0], dtype=jnp.int32)
    return jnp.logical_and(doc_ids[:, None] == doc_ids[None, :], order[None, :] <= order[:, None])


def attend(queries, key_heads, value_heads, doc_ids):
    rows, heads_here, head_width = queries.shape
    shared_heads = key_heads.shape[1]
    grouped_queries = queries.reshape(rows, shared_heads, heads_here // shared_heads, head_width)
    scores = jnp.einsum(
        "qagd,kad->agqk",
        grouped_queries,
        key_heads,
        precision=lax.Precision.HIGHEST,
        preferred_element_type=jnp.float32,
    ) * head_width ** (-0.5)
    scores = jnp.where(visible(doc_ids), scores, jnp.float32(-1e30))
    row_max = jnp.max(scores, axis=-1, keepdims=True)
    spread = jnp.exp(scores - row_max)
    weights = (spread / jnp.sum(spread, axis=-1, keepdims=True)).astype(jnp.bfloat16)
    mixed = jnp.einsum("agqk,kad->qagd", weights, value_heads, preferred_element_type=jnp.float32)
    return mixed.astype(jnp.bfloat16).reshape(rows, heads_here * head_width)


def expand(rows_in, gate_local, up_local):
    gate = jnp.dot(rows_in, gate_local, preferred_element_type=jnp.float32)
    upward = jnp.dot(rows_in, up_local, preferred_element_type=jnp.float32)
    return (jax.nn.silu(gate) * upward).astype(jnp.bfloat16)


def split_pairs(pairs, places, tensor_count):
    rows = pairs.shape[0]
    if tensor_count > KV:
        parity = lax.axis_index("tensor") % 2
        turned = rotate(pairs.reshape(rows, 1, HD), places).reshape(rows, HD)
        mine = jnp.where(parity == 0, turned, pairs)
        partner = swapped(mine.astype(jnp.bfloat16), "tensor", 0).astype(mine.dtype)
        key_heads = jnp.where(parity == 0, mine, partner).reshape(rows, 1, HD)
        value_heads = (
            jnp.where(parity == 0, partner, mine).astype(jnp.bfloat16).reshape(rows, 1, HD)
        )
    else:
        grouped = pairs.reshape(rows, -1, 2, HD)
        key_heads = rotate(grouped[:, :, 0], places)
        value_heads = grouped[:, :, 1].astype(jnp.bfloat16)
    return (key_heads, value_heads)


def run_layer(current, doc_ids, layer_weights):
    (
        query_local,
        pair_local,
        out_local,
        gate_local,
        up_local,
        down_local,
        gain_attention,
        gain_forward,
    ) = layer_weights
    tensor_count = lax.axis_size("tensor")
    micro_rows = doc_ids.shape[0]
    query_cols = query_local.shape[1]
    places = doc_positions(doc_ids)
    piece = lax.all_gather(normalize(current, gain_attention), "tensor", axis=0, tiled=True)
    projected = jnp.concatenate(
        [
            jnp.dot(piece, query_local, preferred_element_type=jnp.float32),
            jnp.dot(piece, pair_local, preferred_element_type=jnp.float32),
        ],
        axis=1,
    )
    heads_here = query_cols // HD
    queries = rotate(projected[:, :query_cols].reshape(micro_rows, heads_here, HD), places)
    key_heads, value_heads = split_pairs(projected[:, query_cols:], places, tensor_count)
    mixed = attend(queries, key_heads, value_heads, doc_ids)
    total = lax.psum_scatter(
        jnp.dot(mixed, out_local, preferred_element_type=jnp.float32).astype(jnp.bfloat16),
        "tensor",
        scatter_dimension=0,
        tiled=True,
    ).astype(jnp.float32)
    halfway = current + total
    hidden = expand(
        lax.all_gather(normalize(halfway, gain_forward), "tensor", axis=0, tiled=True),
        gate_local,
        up_local,
    )
    forward = lax.psum_scatter(
        jnp.dot(hidden, down_local, preferred_element_type=jnp.float32).astype(jnp.bfloat16),
        "tensor",
        scatter_dimension=0,
        tiled=True,
    ).astype(jnp.float32)
    return halfway + forward


def pass_on(result):
    return shifted(result.astype(jnp.bfloat16), "pipe", 1).astype(result.dtype)


def section_kernel(
    first,
    feed_ref,
    before_ref,
    cos_ref,
    sin_ref,
    bias_ref,
    gain_one_ref,
    gain_two_ref,
    query_ref,
    pair_ref,
    out_ref,
    gate_ref,
    up_ref,
    down_ref,
    result_ref,
    x_ref,
    left_buf,
    right_buf,
    tail_buf,
    full_one,
    full_two,
    total,
    outgoing,
    incoming,
    halfway,
    weight_sem,
    send_sem,
    recv_sem,
    pass_send_sem,
    pass_recv_sem,
):
    mine = lax.axis_index("tensor")
    peer = 1 - mine
    phase = lax.axis_index("pipe")
    last = lax.axis_size("pipe") - 1
    rows = feed_ref.shape[0]
    piece = rows // PIECES
    heads_steps = query_ref.shape[1] // CHUNK
    hidden_steps = gate_ref.shape[1] // CHUNK
    my_rows = pl.ds(pl.multiple_of(mine * rows, rows), rows)
    peer_rows = pl.ds(pl.multiple_of(peer * rows, rows), rows)

    def weight_copies(left, right, tail, index, slot):
        cols = pl.ds(pl.multiple_of(index * CHUNK, CHUNK), CHUNK)
        return (
            pltpu.make_async_copy(left.at[:, cols], left_buf.at[slot], weight_sem.at[0, slot]),
            pltpu.make_async_copy(right.at[:, cols], right_buf.at[slot], weight_sem.at[1, slot]),
            pltpu.make_async_copy(tail.at[cols, :], tail_buf.at[slot], weight_sem.at[2, slot]),
        )

    def attention_copies(index, slot):
        return weight_copies(query_ref, pair_ref, out_ref, index, slot)

    def hidden_copies(index, slot):
        return weight_copies(gate_ref, up_ref, down_ref, index, slot)

    for step in range(SLOTS):
        if step < heads_steps:
            copies = attention_copies(step, step)
        else:
            copies = hidden_copies(step - heads_steps, step)
        for copy in copies:
            copy.start()

    barrier = pltpu.get_barrier_semaphore()
    pl.semaphore_signal(
        barrier, inc=1, device_id={"tensor": peer}, device_id_type=pl.DeviceIdType.MESH
    )
    if first:
        pl.semaphore_wait(barrier, 1)
    else:

        @pl.when(phase > 0)
        def _():
            pl.semaphore_signal(
                barrier, inc=1, device_id={"pipe": phase - 1}, device_id_type=pl.DeviceIdType.MESH
            )

        @pl.when(phase < last)
        def _():
            pl.semaphore_wait(barrier, 2)

        @pl.when(phase == last)
        def _():
            pl.semaphore_wait(barrier, 1)

    def pass_copy(index):
        part = pl.ds(index * piece, piece)
        return pltpu.make_async_remote_copy(
            src_ref=before_ref.at[part, :],
            dst_ref=x_ref.at[part, :],
            send_sem=pass_send_sem.at[index],
            recv_sem=pass_recv_sem.at[index],
            device_id={"pipe": lax.rem(phase + 1, last + 1)},
            device_id_type=pl.DeviceIdType.MESH,
        )

    if first:
        x_ref[...] = feed_ref[...]
    else:

        @pl.when(phase < last)
        def _():
            for index in range(PIECES):
                pass_copy(index).start()

        @pl.when(phase == 0)
        def _():
            x_ref[...] = feed_ref[...]

    def send(source, target, index):
        return pltpu.make_async_remote_copy(
            src_ref=source,
            dst_ref=target,
            send_sem=send_sem.at[index],
            recv_sem=recv_sem.at[index],
            device_id={"tensor": peer},
            device_id_type=pl.DeviceIdType.MESH,
        )

    def normed_rows(values, gain):
        meansq = jnp.mean(values * values, axis=-1, keepdims=True)
        return (values * lax.rsqrt(meansq + 1e-05) * gain).astype(jnp.bfloat16)

    def share(source, gain, full, base, arrive):
        copies = []
        for index in range(PIECES):
            if arrive:

                @pl.when(phase > 0)
                def _():
                    pass_copy(index).wait_recv()

            part = pl.ds(index * piece, piece)
            there = pl.ds(pl.multiple_of(mine * rows + index * piece, piece), piece)
            full[there, :] = normed_rows(source[part, :].astype(jnp.float32), gain)
            copy = send(full.at[there, :], full.at[there, :], base + index)
            copy.start()
            copies.append(copy)
        for copy in copies:
            copy.wait()

    def reduce(index):
        outgoing[index] = total[peer_rows, :].astype(jnp.bfloat16)
        copy = send(outgoing.at[index], incoming.at[index], 2 * PIECES + index)
        copy.start()
        copy.wait()
        own = total[my_rows, :].astype(jnp.bfloat16).astype(jnp.float32)
        return own + incoming[index].astype(jnp.float32)

    def rotated(values):
        return values * cos_ref[...] + pltpu.roll(values, HD // 2, 1) * sin_ref[...]

    share(x_ref, gain_one_ref[...], full_one, 0, not first)
    total[...] = jnp.zeros_like(total)

    def attention_step(step, carry):
        slot = lax.rem(step, SLOTS)
        for copy in attention_copies(step, slot):
            copy.wait()
        normed = full_one[...]
        queries = jnp.dot(normed, left_buf[slot], preferred_element_type=jnp.float32)
        pair = jnp.dot(normed, right_buf[slot], preferred_element_type=jnp.float32)
        mixed = []
        for head in range(CHUNK // HD):
            start = head // 2 * 2 * HD
            if head % 2 == 0:
                keys = rotated(pair[:, start : start + HD]).astype(jnp.bfloat16)
                values = pair[:, start + HD : start + 2 * HD].astype(jnp.bfloat16)
            query = rotated(queries[:, head * HD : (head + 1) * HD]).astype(jnp.bfloat16)
            scores = lax.dot_general(
                query, keys, (((1,), (1,)), ((), ())), preferred_element_type=jnp.float32
            )
            scores = scores * HD ** (-0.5) + bias_ref[...]
            spread = jnp.exp(scores - jnp.max(scores, axis=-1, keepdims=True))
            weights = spread / jnp.sum(spread, axis=-1, keepdims=True)
            mixed.append(
                jnp.dot(weights.astype(jnp.bfloat16), values, preferred_element_type=jnp.float32)
            )
        both = jnp.concatenate(mixed, axis=1).astype(jnp.bfloat16)
        total[...] += jnp.dot(both, tail_buf[slot], preferred_element_type=jnp.float32)
        for copy in hidden_copies(step + SLOTS - heads_steps, slot):
            copy.start()
        return carry

    lax.fori_loop(0, heads_steps, attention_step, 0)

    halfway[...] = x_ref[...].astype(jnp.float32) + reduce(0)
    share(halfway, gain_two_ref[...], full_two, PIECES, False)
    total[...] = jnp.zeros_like(total)

    def hidden_step(step, carry):
        slot = lax.rem(step + heads_steps, SLOTS)
        for copy in hidden_copies(step, slot):
            copy.wait()
        normed = full_two[...]
        gate = jnp.dot(normed, left_buf[slot], preferred_element_type=jnp.float32)
        upward = jnp.dot(normed, right_buf[slot], preferred_element_type=jnp.float32)
        hidden = (gate / (1.0 + jnp.exp(-gate)) * upward).astype(jnp.bfloat16)
        total[...] += jnp.dot(hidden, tail_buf[slot], preferred_element_type=jnp.float32)

        @pl.when(step + SLOTS < hidden_steps)
        def _():
            for copy in hidden_copies(step + SLOTS, slot):
                copy.start()

        return carry

    lax.fori_loop(0, hidden_steps, hidden_step, 0)
    result_ref[...] = (halfway[...] + reduce(1)).astype(jnp.bfloat16)
    if not first:

        @pl.when(phase < last)
        def _():
            for index in range(PIECES):
                pass_copy(index).wait_send()


def run_section(feed, before, cosine, sine, bias, layer_weights):
    (
        query_local,
        pair_local,
        out_local,
        gate_local,
        up_local,
        down_local,
        gain_attention,
        gain_forward,
    ) = layer_weights
    rows, width = feed.shape
    first = before is None
    resident = pl.BlockSpec(memory_space=pltpu.VMEM)
    streamed = pl.BlockSpec(memory_space=pl.ANY)
    return pl.pallas_call(
        functools.partial(section_kernel, first),
        out_shape=jax.ShapeDtypeStruct((rows, width), jnp.bfloat16),
        in_specs=[resident] * 7 + [streamed] * 6,
        out_specs=resident,
        scratch_shapes=[
            pltpu.VMEM((rows, width), jnp.bfloat16),
            pltpu.VMEM((SLOTS, width, CHUNK), jnp.bfloat16),
            pltpu.VMEM((SLOTS, width, CHUNK), jnp.bfloat16),
            pltpu.VMEM((SLOTS, CHUNK, width), jnp.bfloat16),
            pltpu.VMEM((2 * rows, width), jnp.bfloat16),
            pltpu.VMEM((2 * rows, width), jnp.bfloat16),
            pltpu.VMEM((2 * rows, width), jnp.float32),
            pltpu.VMEM((2, rows, width), jnp.bfloat16),
            pltpu.VMEM((2, rows, width), jnp.bfloat16),
            pltpu.VMEM((rows, width), jnp.float32),
            pltpu.SemaphoreType.DMA((3, SLOTS)),
            pltpu.SemaphoreType.DMA((2 * PIECES + 2,)),
            pltpu.SemaphoreType.DMA((2 * PIECES + 2,)),
            pltpu.SemaphoreType.DMA((PIECES,)),
            pltpu.SemaphoreType.DMA((PIECES,)),
        ],
        compiler_params=pltpu.CompilerParams(
            collective_id=0 if first else 1, has_side_effects=True, vmem_limit_bytes=60 * 2**20
        ),
        cost_estimate=pl.CostEstimate(
            flops=2 * 2 * rows * 5 * 256 * width * 12,
            bytes_accessed=5 * 256 * width * 24,
            transcendentals=0,
        ),
    )(
        feed,
        feed if first else before,
        cosine,
        sine,
        bias,
        gain_attention[None, :],
        gain_forward[None, :],
        query_local,
        pair_local,
        out_local,
        gate_local,
        up_local,
        down_local,
    )


def regroup(tokens, destination, micro_count, micro_rows):
    group_count = lax.axis_size("dp")
    slab_rows = micro_rows // lax.axis_size("tensor")
    held_rows, width = tokens.shape
    capacity = held_rows // 2
    group_span = micro_count * micro_rows
    groups = jnp.arange(group_count, dtype=jnp.int32)
    order = jnp.arange(held_rows, dtype=jnp.int32)
    target = destination // group_span
    within = destination % group_span
    landing = within // micro_rows * slab_rows + within % slab_rows
    member = (target[None, :] == groups[:, None]).astype(jnp.float32)
    earlier = (order[:, None] < order[None, :]).astype(jnp.bfloat16)
    counts = jnp.dot(member.astype(jnp.bfloat16), earlier, preferred_element_type=jnp.float32)
    before = jnp.sum(counts * member, axis=0).astype(jnp.int32)
    slots = jnp.arange(group_count * capacity, dtype=jnp.int32)
    pack = (slots[:, None] == (target * capacity + before)[None, :]).astype(jnp.bfloat16)
    column = jnp.arange(HD, dtype=jnp.int32)[None, :]
    notes = jnp.where(
        column == 0,
        (landing // HD + 1)[:, None],
        jnp.where(column == 1, (landing % HD)[:, None], 0),
    ).astype(jnp.bfloat16)
    send_rows = jnp.dot(
        pack, jnp.concatenate([tokens, notes], axis=1), preferred_element_type=jnp.float32
    ).astype(jnp.bfloat16)
    got_rows = lax.all_to_all(
        send_rows.reshape(group_count, capacity, width + HD),
        "dp",
        split_axis=0,
        concat_axis=0,
        tiled=True,
    ).reshape(-1, width + HD)
    marks = got_rows[:, width : width + 2].astype(jnp.int32)
    lands = (marks[:, 0] - 1) * HD + marks[:, 1]
    unpack = (order[:, None] == lands[None, :]).astype(jnp.bfloat16)
    return jnp.dot(unpack, got_rows[:, :width], preferred_element_type=jnp.float32).astype(
        jnp.bfloat16
    )


def section_tables(doc_ids):
    group, micro_rows = doc_ids.shape
    tensor_count = lax.axis_size("tensor")

    def laid(table):
        by_slab = table.reshape(group, tensor_count, micro_rows // tensor_count)
        return jnp.swapaxes(by_slab, 0, 1).reshape(-1)

    places = laid(jax.vmap(doc_positions)(doc_ids))
    order = laid(jnp.broadcast_to(jnp.arange(micro_rows, dtype=jnp.int32), doc_ids.shape))
    batch = laid(jnp.broadcast_to(jnp.arange(group, dtype=jnp.int32)[:, None], doc_ids.shape))
    docs = laid(doc_ids)
    shown = (
        (docs[:, None] == docs[None, :])
        & (batch[:, None] == batch[None, :])
        & (order[None, :] <= order[:, None])
    )
    bias = jnp.where(shown, jnp.float32(0), jnp.float32(-1e30))
    frequency = 500000.0 ** (-(jnp.arange(HD // 2, dtype=jnp.float32) * 2.0 / HD))
    angles = places[:, None] * frequency[None, :]
    cosine, sine = jnp.cos(angles), jnp.sin(angles)
    return (
        jnp.concatenate([cosine, cosine], axis=1),
        jnp.concatenate([-sine, sine], axis=1),
        bias,
    )


def paired_shards(tokens, destination, segments, layer_weights):
    pipe_count = lax.axis_size("pipe")
    micro_count, micro_rows = segments.shape
    slab_rows = micro_rows // lax.axis_size("tensor")
    width = tokens.shape[1]
    group = 2
    group_rows = group * slab_rows
    rounds = micro_count // group
    regrouped = regroup(tokens, destination, micro_count, micro_rows)
    phase_index = lax.axis_index("pipe")
    tables = [section_tables(segments[r * group : (r + 1) * group]) for r in range(rounds)]
    result = None
    mine = jnp.zeros((slab_rows, width), jnp.bfloat16)
    for moment in range(rounds + pipe_count - 1):
        feed = min(moment, rounds - 1)
        current = regrouped[feed * group_rows : (feed + 1) * group_rows]
        round_index = jnp.clip(moment - phase_index, 0, rounds - 1)
        cosine, sine, bias = (
            lax.select_n(round_index, *[table[i] for table in tables]) for i in range(3)
        )
        result = run_section(current, result, cosine, sine, bias, layer_weights)
        done = moment - (pipe_count - 1)
        if done >= 0:
            for inner in range(group):
                piece = result[inner * slab_rows : (inner + 1) * slab_rows]
                home = done * group + inner
                if home != pipe_count - 1:
                    piece = lax.ppermute(piece, "pipe", [(pipe_count - 1, home)])
                mine = jnp.where(phase_index == home, piece, mine)
    return mine.astype(jnp.float32)


def shards(
    tokens,
    destination,
    segments,
    query_weight,
    key_value_weight,
    out_weight,
    gate_weight,
    up_weight,
    down_weight,
    attention_gain,
    forward_gain,
):
    if lax.axis_size("tensor") == 2:
        layer_weights = (
            query_weight[0],
            key_value_weight[0],
            out_weight[0],
            gate_weight[0],
            up_weight[0],
            down_weight[0],
            attention_gain[0],
            forward_gain[0],
        )
        return paired_shards(tokens, destination, segments, layer_weights)
    group_count = lax.axis_size("dp")
    tensor_count = lax.axis_size("tensor")
    pipe_count = lax.axis_size("pipe")
    micro_count, micro_rows = segments.shape
    slab_rows = micro_rows // tensor_count
    held_rows, width = tokens.shape
    capacity = held_rows // 2
    group_span = micro_count * micro_rows
    target = destination // group_span
    within = destination % group_span
    landing = within // micro_rows * slab_rows + within % slab_rows
    member = (target[:, None] == jnp.arange(group_count, dtype=jnp.int32)[None, :]).astype(
        jnp.int32
    )
    before = jnp.sum((jnp.cumsum(member, axis=0) - member) * member, axis=1)
    slot_index = target * capacity + before
    send_rows = jnp.zeros((group_count * capacity, width), jnp.bfloat16).at[slot_index].set(tokens)
    send_places = (
        jnp.full((group_count * capacity,), held_rows, jnp.int32).at[slot_index].set(landing)
    )
    got_rows, got_places = (
        lax.all_to_all(
            send_rows.reshape(group_count, capacity, width),
            "dp",
            split_axis=0,
            concat_axis=0,
            tiled=True,
        ),
        lax.all_to_all(
            send_places.reshape(group_count, capacity),
            "dp",
            split_axis=0,
            concat_axis=0,
            tiled=True,
        ),
    )
    regrouped = (
        jnp.zeros((held_rows, width), jnp.bfloat16)
        .at[got_places.reshape(-1)]
        .set(got_rows.reshape(-1, width), mode="drop")
    )
    micro_batches = regrouped.reshape(micro_count, slab_rows, width)
    layer_weights = (
        query_weight[0],
        key_value_weight[0],
        out_weight[0],
        gate_weight[0],
        up_weight[0],
        down_weight[0],
        attention_gain[0],
        forward_gain[0],
    )
    phase_index = lax.axis_index("pipe")
    carried = jnp.zeros((slab_rows, width), jnp.float32)
    finished = []
    for moment in range(micro_count + pipe_count - 1):
        feed_rows = micro_batches[min(moment, micro_count - 1)].astype(jnp.float32)
        current = jnp.where(
            jnp.logical_and(phase_index == 0, moment < micro_count), feed_rows, carried
        )
        micro_index = jnp.clip(moment - phase_index, 0, micro_count - 1)
        doc_ids = lax.dynamic_index_in_dim(segments, micro_index, 0, keepdims=False)
        result = run_layer(current, doc_ids, layer_weights)
        if moment >= pipe_count - 1:
            finished.append(result)
        if moment < micro_count + pipe_count - 2:
            carried = pass_on(result)
    everyone = broadcast(jnp.stack(finished).astype(jnp.bfloat16), "pipe", pipe_count - 1).astype(
        jnp.float32
    )
    return lax.dynamic_index_in_dim(everyone, phase_index, 0, keepdims=False)


def solution(mesh):
    placed = (
        P(("dp", "tensor"), None),
        P(("dp", "tensor")),
        P("dp", None),
        P("pipe", None, "tensor"),
        P("pipe", None, "tensor"),
        P("pipe", "tensor", None),
        P("pipe", None, "tensor"),
        P("pipe", None, "tensor"),
        P("pipe", "tensor", None),
        P("pipe", None),
        P("pipe", None),
    )
    return jax.shard_map(
        shards,
        mesh=mesh,
        in_specs=placed,
        out_specs=P(("dp", "pipe", "tensor"), None),
        check_vma=False,
    )
```

```python
import functools

import jax
import jax.numpy as jnp
from jax import lax
from jax.experimental import pallas as pl
from jax.experimental.pallas import tpu as pltpu
from jax.sharding import PartitionSpec as P

KV = 8
HD = 128
SLOTS = 3
CHUNK = 512
PIECES = 4


def swapped(value, axis, apart):
    mask = 2**apart
    pairs = [(source, source ^ mask) for source in range(lax.axis_size(axis))]
    return lax.ppermute(value, axis, pairs)


def shifted(array, axis, by):
    peers = lax.axis_size(axis)
    pairs = [(i, i + by) for i in range(peers) if 0 <= i + by < peers]
    return lax.ppermute(array, axis, pairs)


def broadcast(block, axis, source):
    block = jnp.where(lax.axis_index(axis) == source, block, jnp.zeros_like(block))
    return lax.psum(block, axis)


def doc_positions(doc_ids):
    order = jnp.arange(doc_ids.shape[0], dtype=jnp.int32)
    change = jnp.concatenate([jnp.ones((1,), dtype=bool), doc_ids[1:] != doc_ids[:-1]])
    starts = lax.cummax(jnp.where(change, order, jnp.zeros_like(order)), axis=0)
    return (order - starts).astype(jnp.float32)


def rotate(stack, places):
    half_width = stack.shape[-1] // 2
    frequency = 500000.0 ** (-(jnp.arange(half_width, dtype=jnp.float32) * 2.0 / stack.shape[-1]))
    angles = places[:, None] * frequency[None, :]
    cosine = jnp.cos(angles)[:, None, :]
    sine_part = jnp.sin(angles)[:, None, :]
    front_half = stack[..., :half_width]
    back_half = stack[..., half_width:]
    return jnp.concatenate(
        [front_half * cosine - back_half * sine_part, back_half * cosine + front_half * sine_part],
        axis=-1,
    )


def normalize(rows_in, gain):
    meansq = jnp.mean(rows_in * rows_in, axis=-1, keepdims=True)
    return (rows_in * lax.rsqrt(meansq + 1e-05) * gain).astype(jnp.bfloat16)


def visible(doc_ids):
    order = jnp.arange(doc_ids.shape[0], dtype=jnp.int32)
    return jnp.logical_and(doc_ids[:, None] == doc_ids[None, :], order[None, :] <= order[:, None])


def attend(queries, key_heads, value_heads, doc_ids):
    rows, heads_here, head_width = queries.shape
    shared_heads = key_heads.shape[1]
    grouped_queries = queries.reshape(rows, shared_heads, heads_here // shared_heads, head_width)
    scores = jnp.einsum(
        "qagd,kad->agqk",
        grouped_queries,
        key_heads,
        precision=lax.Precision.HIGHEST,
        preferred_element_type=jnp.float32,
    ) * head_width ** (-0.5)
    scores = jnp.where(visible(doc_ids), scores, jnp.float32(-1e30))
    row_max = jnp.max(scores, axis=-1, keepdims=True)
    spread = jnp.exp(scores - row_max)
    weights = (spread / jnp.sum(spread, axis=-1, keepdims=True)).astype(jnp.bfloat16)
    mixed = jnp.einsum("agqk,kad->qagd", weights, value_heads, preferred_element_type=jnp.float32)
    return mixed.astype(jnp.bfloat16).reshape(rows, heads_here * head_width)


def expand(rows_in, gate_local, up_local):
    gate = jnp.dot(rows_in, gate_local, preferred_element_type=jnp.float32)
    upward = jnp.dot(rows_in, up_local, preferred_element_type=jnp.float32)
    return (jax.nn.silu(gate) * upward).astype(jnp.bfloat16)


def split_pairs(pairs, places, tensor_count):
    rows = pairs.shape[0]
    if tensor_count > KV:
        parity = lax.axis_index("tensor") % 2
        turned = rotate(pairs.reshape(rows, 1, HD), places).reshape(rows, HD)
        mine = jnp.where(parity == 0, turned, pairs)
        partner = swapped(mine.astype(jnp.bfloat16), "tensor", 0).astype(mine.dtype)
        key_heads = jnp.where(parity == 0, mine, partner).reshape(rows, 1, HD)
        value_heads = (
            jnp.where(parity == 0, partner, mine).astype(jnp.bfloat16).reshape(rows, 1, HD)
        )
    else:
        grouped = pairs.reshape(rows, -1, 2, HD)
        key_heads = rotate(grouped[:, :, 0], places)
        value_heads = grouped[:, :, 1].astype(jnp.bfloat16)
    return (key_heads, value_heads)


def run_layer(current, doc_ids, layer_weights):
    (
        query_local,
        pair_local,
        out_local,
        gate_local,
        up_local,
        down_local,
        gain_attention,
        gain_forward,
    ) = layer_weights
    tensor_count = lax.axis_size("tensor")
    micro_rows = doc_ids.shape[0]
    query_cols = query_local.shape[1]
    places = doc_positions(doc_ids)
    piece = lax.all_gather(normalize(current, gain_attention), "tensor", axis=0, tiled=True)
    projected = jnp.concatenate(
        [
            jnp.dot(piece, query_local, preferred_element_type=jnp.float32),
            jnp.dot(piece, pair_local, preferred_element_type=jnp.float32),
        ],
        axis=1,
    )
    heads_here = query_cols // HD
    queries = rotate(projected[:, :query_cols].reshape(micro_rows, heads_here, HD), places)
    key_heads, value_heads = split_pairs(projected[:, query_cols:], places, tensor_count)
    mixed = attend(queries, key_heads, value_heads, doc_ids)
    total = lax.psum_scatter(
        jnp.dot(mixed, out_local, preferred_element_type=jnp.float32).astype(jnp.bfloat16),
        "tensor",
        scatter_dimension=0,
        tiled=True,
    ).astype(jnp.float32)
    halfway = current + total
    hidden = expand(
        lax.all_gather(normalize(halfway, gain_forward), "tensor", axis=0, tiled=True),
        gate_local,
        up_local,
    )
    forward = lax.psum_scatter(
        jnp.dot(hidden, down_local, preferred_element_type=jnp.float32).astype(jnp.bfloat16),
        "tensor",
        scatter_dimension=0,
        tiled=True,
    ).astype(jnp.float32)
    return halfway + forward


def pass_on(result):
    return shifted(result.astype(jnp.bfloat16), "pipe", 1).astype(result.dtype)


def section_kernel(
    final,
    x_ref,
    before_ref,
    cos_ref,
    sin_ref,
    bias_ref,
    gain_one_ref,
    gain_two_ref,
    query_ref,
    pair_ref,
    out_ref,
    gate_ref,
    up_ref,
    down_ref,
    result_ref,
    landed_ref,
    left_buf,
    right_buf,
    out_buf,
    down_buf,
    hidden_buf,
    full_one,
    full_two,
    total,
    outgoing,
    incoming,
    halfway,
    weight_sem,
    out_sem,
    down_sem,
    part_send_sem,
    part_recv_sem,
    send_sem,
    recv_sem,
    pass_send_sem,
    pass_recv_sem,
):
    mine = lax.axis_index("tensor")
    peer = 1 - mine
    phase = lax.axis_index("pipe")
    last = lax.axis_size("pipe") - 1
    rows = x_ref.shape[0]
    blocks = down_ref.shape[1] // CHUNK
    piece = rows // PIECES
    heads_steps = query_ref.shape[1] // CHUNK
    hidden_steps = gate_ref.shape[1] // CHUNK
    my_rows = pl.ds(pl.multiple_of(mine * rows, rows), rows)
    peer_rows = pl.ds(pl.multiple_of(peer * rows, rows), rows)

    def columns(index):
        return pl.ds(pl.multiple_of(index * CHUNK, CHUNK), CHUNK)

    def weight_copies(left, right, index, slot):
        cols = columns(index)
        return (
            pltpu.make_async_copy(left.at[:, cols], left_buf.at[slot], weight_sem.at[0, slot]),
            pltpu.make_async_copy(right.at[:, cols], right_buf.at[slot], weight_sem.at[1, slot]),
        )

    def attention_copies(index, slot):
        return weight_copies(query_ref, pair_ref, index, slot)

    def hidden_copies(index, slot):
        return weight_copies(gate_ref, up_ref, index, slot)

    def out_copy(index):
        return pltpu.make_async_copy(
            out_ref.at[columns(index), :], out_buf.at[index], out_sem.at[index]
        )

    def down_copy(index, slot):
        return pltpu.make_async_copy(
            down_ref.at[:, columns(index)], down_buf.at[slot], down_sem.at[slot]
        )

    for step in range(heads_steps):
        for copy in attention_copies(step, step):
            copy.start()
        out_copy(step).start()
    for step in range(heads_steps, SLOTS):
        for copy in hidden_copies(step - heads_steps, step):
            copy.start()
    for step in range(SLOTS):
        down_copy(step, step).start()

    barrier = pltpu.get_barrier_semaphore()
    pl.semaphore_signal(
        barrier, inc=1, device_id={"tensor": peer}, device_id_type=pl.DeviceIdType.MESH
    )
    pipe_signals = [(phase < 2, last)] if final else [(phase > 0, phase - 1)]
    for sends, there in pipe_signals:

        @pl.when(sends)
        def _():
            pl.semaphore_signal(
                barrier, inc=1, device_id={"pipe": there}, device_id_type=pl.DeviceIdType.MESH
            )

    greeted = phase == last if final else phase < last

    @pl.when(greeted)
    def _():
        pl.semaphore_wait(barrier, 3 if final else 2)

    @pl.when(jnp.logical_not(greeted))
    def _():
        pl.semaphore_wait(barrier, 1)

    def pass_copy(index):
        cols = columns(index)
        return pltpu.make_async_remote_copy(
            src_ref=result_ref.at[:, cols],
            dst_ref=landed_ref.at[:, cols],
            send_sem=pass_send_sem.at[index],
            recv_sem=pass_recv_sem.at[index],
            device_id={"pipe": lax.rem(phase + 1, last + 1)},
            device_id_type=pl.DeviceIdType.MESH,
        )

    def exit_copy(home):
        half = rows // 2
        return pltpu.make_async_remote_copy(
            src_ref=before_ref.at[pl.ds(home * half, half), :],
            dst_ref=landed_ref,
            send_sem=pass_send_sem.at[home],
            recv_sem=pass_recv_sem.at[0],
            device_id={"pipe": home},
            device_id_type=pl.DeviceIdType.MESH,
        )

    if final:

        @pl.when(phase == last)
        def _():
            for home in range(2):
                exit_copy(home).start()

    def send(source, target, index):
        return pltpu.make_async_remote_copy(
            src_ref=source,
            dst_ref=target,
            send_sem=send_sem.at[index],
            recv_sem=recv_sem.at[index],
            device_id={"tensor": peer},
            device_id_type=pl.DeviceIdType.MESH,
        )

    def normed_rows(values, gain):
        meansq = jnp.mean(values * values, axis=-1, keepdims=True)
        return (values * lax.rsqrt(meansq + 1e-05) * gain).astype(jnp.bfloat16)

    def share(source, gain, full, base):
        copies = []
        for index in range(PIECES):
            part = pl.ds(index * piece, piece)
            there = pl.ds(pl.multiple_of(mine * rows + index * piece, piece), piece)
            full[there, :] = normed_rows(source[part, :].astype(jnp.float32), gain)
            copy = send(full.at[there, :], full.at[there, :], base + index)
            copy.start()
            copies.append(copy)
        for copy in copies:
            copy.wait()

    def reduce():
        outgoing[0] = total[peer_rows, :].astype(jnp.bfloat16)
        copy = send(outgoing.at[0], incoming.at[0], 2 * PIECES)
        copy.start()
        copy.wait()
        own = total[my_rows, :].astype(jnp.bfloat16).astype(jnp.float32)
        return own + incoming[0].astype(jnp.float32)

    def part_copy(index):
        cols = columns(index)
        return pltpu.make_async_remote_copy(
            src_ref=outgoing.at[1, :, cols],
            dst_ref=incoming.at[1, :, cols],
            send_sem=part_send_sem.at[index],
            recv_sem=part_recv_sem.at[index],
            device_id={"tensor": peer},
            device_id_type=pl.DeviceIdType.MESH,
        )

    def finish(index):
        cols = columns(index)
        part_copy(index).wait()
        own = total[my_rows, cols].astype(jnp.bfloat16).astype(jnp.float32)
        summed = own + incoming[1, :, cols].astype(jnp.float32)
        result_ref[:, cols] = (halfway[:, cols] + summed).astype(jnp.bfloat16)
        if not final:

            @pl.when(phase < last)
            def _():
                pass_copy(index).start()

    def rotated(values):
        return values * cos_ref[...] + pltpu.roll(values, HD // 2, 1) * sin_ref[...]

    share(x_ref, gain_one_ref[...], full_one, 0)
    total[...] = jnp.zeros_like(total)

    def attention_step(step, carry):
        slot = lax.rem(step, SLOTS)
        for copy in attention_copies(step, slot):
            copy.wait()
        out_copy(step).wait()
        normed = full_one[...]
        queries = jnp.dot(normed, left_buf[slot], preferred_element_type=jnp.float32)
        pair = jnp.dot(normed, right_buf[slot], preferred_element_type=jnp.float32)
        mixed = []
        for head in range(CHUNK // HD):
            start = head // 2 * 2 * HD
            if head % 2 == 0:
                keys = rotated(pair[:, start : start + HD]).astype(jnp.bfloat16)
                values = pair[:, start + HD : start + 2 * HD].astype(jnp.bfloat16)
            query = rotated(queries[:, head * HD : (head + 1) * HD]).astype(jnp.bfloat16)
            scores = lax.dot_general(
                query, keys, (((1,), (1,)), ((), ())), preferred_element_type=jnp.float32
            )
            scores = scores * HD ** (-0.5) + bias_ref[...]
            spread = jnp.exp(scores - jnp.max(scores, axis=-1, keepdims=True))
            weights = spread / jnp.sum(spread, axis=-1, keepdims=True)
            mixed.append(
                jnp.dot(weights.astype(jnp.bfloat16), values, preferred_element_type=jnp.float32)
            )
        both = jnp.concatenate(mixed, axis=1).astype(jnp.bfloat16)
        total[...] += jnp.dot(both, out_buf[step], preferred_element_type=jnp.float32)
        for copy in hidden_copies(step + SLOTS - heads_steps, slot):
            copy.start()
        return carry

    lax.fori_loop(0, heads_steps, attention_step, 0)

    halfway[...] = x_ref[...].astype(jnp.float32) + reduce()
    share(halfway, gain_two_ref[...], full_two, PIECES)

    def hidden_step(step, carry):
        slot = lax.rem(step + heads_steps, SLOTS)
        for copy in hidden_copies(step, slot):
            copy.wait()
        normed = full_two[...]
        gate = jnp.dot(normed, left_buf[slot], preferred_element_type=jnp.float32)
        upward = jnp.dot(normed, right_buf[slot], preferred_element_type=jnp.float32)
        hidden = gate / (1.0 + jnp.exp(-gate)) * upward
        hidden_buf[:, columns(step)] = hidden.astype(jnp.bfloat16)

        @pl.when(step + SLOTS < hidden_steps)
        def _():
            for copy in hidden_copies(step + SLOTS, slot):
                copy.start()

        return carry

    lax.fori_loop(0, hidden_steps, hidden_step, 0)

    def down_step(step, carry):
        slot = lax.rem(step, SLOTS)
        cols = columns(step)
        down_copy(step, slot).wait()
        total[:, cols] = jnp.dot(
            hidden_buf[...], down_buf[slot], preferred_element_type=jnp.float32
        )
        outgoing[1, :, cols] = total[peer_rows, cols].astype(jnp.bfloat16)
        part_copy(step).start()

        @pl.when(step + SLOTS < blocks)
        def _():
            down_copy(step + SLOTS, slot).start()

        @pl.when(step > 0)
        def _():
            finish(step - 1)

        return carry

    lax.fori_loop(0, blocks, down_step, 0)
    finish(blocks - 1)
    if final:

        @pl.when(phase == last)
        def _():
            for home in range(2):
                exit_copy(home).wait_send()

        @pl.when(phase < 2)
        def _():
            exit_copy(0).wait_recv()

    else:

        @pl.when(phase < last)
        def _():
            for index in range(blocks):
                pass_copy(index).wait_send()

        @pl.when(phase > 0)
        def _():
            for index in range(blocks):
                pass_copy(index).wait_recv()


def run_section(final, current, before, cosine, sine, bias, layer_weights):
    (
        query_local,
        pair_local,
        out_local,
        gate_local,
        up_local,
        down_local,
        gain_attention,
        gain_forward,
    ) = layer_weights
    rows, width = current.shape
    hidden_width = down_local.shape[0]
    blocks = width // CHUNK
    resident = pl.BlockSpec(memory_space=pltpu.VMEM)
    streamed = pl.BlockSpec(memory_space=pl.ANY)
    return pl.pallas_call(
        functools.partial(section_kernel, final),
        out_shape=(
            jax.ShapeDtypeStruct((rows, width), jnp.bfloat16),
            jax.ShapeDtypeStruct((rows // 2 if final else rows, width), jnp.bfloat16),
        ),
        in_specs=[resident] * 7 + [streamed] * 6,
        out_specs=(resident, resident),
        scratch_shapes=[
            pltpu.VMEM((SLOTS, width, CHUNK), jnp.bfloat16),
            pltpu.VMEM((SLOTS, width, CHUNK), jnp.bfloat16),
            pltpu.VMEM((out_local.shape[0] // CHUNK, CHUNK, width), jnp.bfloat16),
            pltpu.VMEM((SLOTS, hidden_width, CHUNK), jnp.bfloat16),
            pltpu.VMEM((2 * rows, hidden_width), jnp.bfloat16),
            pltpu.VMEM((2 * rows, width), jnp.bfloat16),
            pltpu.VMEM((2 * rows, width), jnp.bfloat16),
            pltpu.VMEM((2 * rows, width), jnp.float32),
            pltpu.VMEM((2, rows, width), jnp.bfloat16),
            pltpu.VMEM((2, rows, width), jnp.bfloat16),
            pltpu.VMEM((rows, width), jnp.float32),
            pltpu.SemaphoreType.DMA((2, SLOTS)),
            pltpu.SemaphoreType.DMA((out_local.shape[0] // CHUNK,)),
            pltpu.SemaphoreType.DMA((SLOTS,)),
            pltpu.SemaphoreType.DMA((blocks,)),
            pltpu.SemaphoreType.DMA((blocks,)),
            pltpu.SemaphoreType.DMA((2 * PIECES + 1,)),
            pltpu.SemaphoreType.DMA((2 * PIECES + 1,)),
            pltpu.SemaphoreType.DMA((blocks,)),
            pltpu.SemaphoreType.DMA((blocks,)),
        ],
        compiler_params=pltpu.CompilerParams(
            collective_id=1 if final else 0, has_side_effects=True, vmem_limit_bytes=60 * 2**20
        ),
        cost_estimate=pl.CostEstimate(
            flops=2 * 2 * rows * 5 * 256 * width * 12,
            bytes_accessed=5 * 256 * width * 24,
            transcendentals=0,
        ),
    )(
        current,
        before,
        cosine,
        sine,
        bias,
        gain_attention[None, :],
        gain_forward[None, :],
        query_local,
        pair_local,
        out_local,
        gate_local,
        up_local,
        down_local,
    )


def regroup(tokens, destination, micro_count, micro_rows):
    group_count = lax.axis_size("dp")
    slab_rows = micro_rows // lax.axis_size("tensor")
    held_rows, width = tokens.shape
    capacity = held_rows // 2
    group_span = micro_count * micro_rows
    groups = jnp.arange(group_count, dtype=jnp.int32)
    order = jnp.arange(held_rows, dtype=jnp.int32)
    target = destination // group_span
    within = destination % group_span
    landing = within // micro_rows * slab_rows + within % slab_rows
    member = (target[None, :] == groups[:, None]).astype(jnp.float32)
    earlier = (order[:, None] < order[None, :]).astype(jnp.bfloat16)
    counts = jnp.dot(member.astype(jnp.bfloat16), earlier, preferred_element_type=jnp.float32)
    before = jnp.sum(counts * member, axis=0).astype(jnp.int32)
    slots = jnp.arange(group_count * capacity, dtype=jnp.int32)
    pack = (slots[:, None] == (target * capacity + before)[None, :]).astype(jnp.bfloat16)
    column = jnp.arange(HD, dtype=jnp.int32)[None, :]
    notes = jnp.where(
        column == 0,
        (landing // HD + 1)[:, None],
        jnp.where(column == 1, (landing % HD)[:, None], 0),
    ).astype(jnp.bfloat16)
    send_rows = jnp.dot(
        pack, jnp.concatenate([tokens, notes], axis=1), preferred_element_type=jnp.float32
    ).astype(jnp.bfloat16)
    got_rows = lax.all_to_all(
        send_rows.reshape(group_count, capacity, width + HD),
        "dp",
        split_axis=0,
        concat_axis=0,
        tiled=True,
    ).reshape(-1, width + HD)
    marks = got_rows[:, width : width + 2].astype(jnp.int32)
    lands = (marks[:, 0] - 1) * HD + marks[:, 1]
    unpack = (order[:, None] == lands[None, :]).astype(jnp.bfloat16)
    return jnp.dot(unpack, got_rows[:, :width], preferred_element_type=jnp.float32).astype(
        jnp.bfloat16
    )


def section_tables(doc_ids):
    group, micro_rows = doc_ids.shape
    tensor_count = lax.axis_size("tensor")

    def laid(table):
        by_slab = table.reshape(group, tensor_count, micro_rows // tensor_count)
        return jnp.swapaxes(by_slab, 0, 1).reshape(-1)

    places = laid(jax.vmap(doc_positions)(doc_ids))
    order = laid(jnp.broadcast_to(jnp.arange(micro_rows, dtype=jnp.int32), doc_ids.shape))
    batch = laid(jnp.broadcast_to(jnp.arange(group, dtype=jnp.int32)[:, None], doc_ids.shape))
    docs = laid(doc_ids)
    shown = (
        (docs[:, None] == docs[None, :])
        & (batch[:, None] == batch[None, :])
        & (order[None, :] <= order[:, None])
    )
    bias = jnp.where(shown, jnp.float32(0), jnp.float32(-1e30))
    frequency = 500000.0 ** (-(jnp.arange(HD // 2, dtype=jnp.float32) * 2.0 / HD))
    angles = places[:, None] * frequency[None, :]
    cosine, sine = jnp.cos(angles), jnp.sin(angles)
    return (
        jnp.concatenate([cosine, cosine], axis=1),
        jnp.concatenate([-sine, sine], axis=1),
        bias,
    )


def paired_shards(tokens, destination, segments, layer_weights):
    pipe_count = lax.axis_size("pipe")
    micro_count, micro_rows = segments.shape
    slab_rows = micro_rows // lax.axis_size("tensor")
    width = tokens.shape[1]
    group = 2
    group_rows = group * slab_rows
    rounds = micro_count // group
    regrouped = regroup(tokens, destination, micro_count, micro_rows)
    phase_index = lax.axis_index("pipe")
    tables = [section_tables(segments[r * group : (r + 1) * group]) for r in range(rounds)]
    result, carried = None, None
    for moment in range(rounds + pipe_count - 1):
        feed = min(moment, rounds - 1)
        current = regrouped[feed * group_rows : (feed + 1) * group_rows]
        if moment > 0:
            current = jnp.where(phase_index == 0, current, carried)
        round_index = jnp.clip(moment - phase_index, 0, rounds - 1)
        cosine, sine, bias = (
            lax.select_n(round_index, *[table[i] for table in tables]) for i in range(3)
        )
        final = moment == rounds + pipe_count - 2
        result, carried = run_section(
            final, current, result if final else current, cosine, sine, bias, layer_weights
        )
    sent = lax.ppermute(result[:slab_rows], "pipe", [(pipe_count - 1, pipe_count - 2)])
    mine = jnp.where(
        phase_index == pipe_count - 1,
        result[slab_rows:],
        jnp.where(phase_index == pipe_count - 2, sent, carried),
    )
    return mine.astype(jnp.float32)


def shards(
    tokens,
    destination,
    segments,
    query_weight,
    key_value_weight,
    out_weight,
    gate_weight,
    up_weight,
    down_weight,
    attention_gain,
    forward_gain,
):
    if lax.axis_size("tensor") == 2 and lax.axis_size("pipe") == segments.shape[0] == 4:
        layer_weights = (
            query_weight[0],
            key_value_weight[0],
            out_weight[0],
            gate_weight[0],
            up_weight[0],
            down_weight[0],
            attention_gain[0],
            forward_gain[0],
        )
        return paired_shards(tokens, destination, segments, layer_weights)
    group_count = lax.axis_size("dp")
    tensor_count = lax.axis_size("tensor")
    pipe_count = lax.axis_size("pipe")
    micro_count, micro_rows = segments.shape
    slab_rows = micro_rows // tensor_count
    held_rows, width = tokens.shape
    capacity = held_rows // 2
    group_span = micro_count * micro_rows
    target = destination // group_span
    within = destination % group_span
    landing = within // micro_rows * slab_rows + within % slab_rows
    member = (target[:, None] == jnp.arange(group_count, dtype=jnp.int32)[None, :]).astype(
        jnp.int32
    )
    before = jnp.sum((jnp.cumsum(member, axis=0) - member) * member, axis=1)
    slot_index = target * capacity + before
    send_rows = jnp.zeros((group_count * capacity, width), jnp.bfloat16).at[slot_index].set(tokens)
    send_places = (
        jnp.full((group_count * capacity,), held_rows, jnp.int32).at[slot_index].set(landing)
    )
    got_rows, got_places = (
        lax.all_to_all(
            send_rows.reshape(group_count, capacity, width),
            "dp",
            split_axis=0,
            concat_axis=0,
            tiled=True,
        ),
        lax.all_to_all(
            send_places.reshape(group_count, capacity),
            "dp",
            split_axis=0,
            concat_axis=0,
            tiled=True,
        ),
    )
    regrouped = (
        jnp.zeros((held_rows, width), jnp.bfloat16)
        .at[got_places.reshape(-1)]
        .set(got_rows.reshape(-1, width), mode="drop")
    )
    micro_batches = regrouped.reshape(micro_count, slab_rows, width)
    layer_weights = (
        query_weight[0],
        key_value_weight[0],
        out_weight[0],
        gate_weight[0],
        up_weight[0],
        down_weight[0],
        attention_gain[0],
        forward_gain[0],
    )
    phase_index = lax.axis_index("pipe")
    carried = jnp.zeros((slab_rows, width), jnp.float32)
    finished = []
    for moment in range(micro_count + pipe_count - 1):
        feed_rows = micro_batches[min(moment, micro_count - 1)].astype(jnp.float32)
        current = jnp.where(
            jnp.logical_and(phase_index == 0, moment < micro_count), feed_rows, carried
        )
        micro_index = jnp.clip(moment - phase_index, 0, micro_count - 1)
        doc_ids = lax.dynamic_index_in_dim(segments, micro_index, 0, keepdims=False)
        result = run_layer(current, doc_ids, layer_weights)
        if moment >= pipe_count - 1:
            finished.append(result)
        if moment < micro_count + pipe_count - 2:
            carried = pass_on(result)
    everyone = broadcast(jnp.stack(finished).astype(jnp.bfloat16), "pipe", pipe_count - 1).astype(
        jnp.float32
    )
    return lax.dynamic_index_in_dim(everyone, phase_index, 0, keepdims=False)


def solution(mesh):
    placed = (
        P(("dp", "tensor"), None),
        P(("dp", "tensor")),
        P("dp", None),
        P("pipe", None, "tensor"),
        P("pipe", None, "tensor"),
        P("pipe", "tensor", None),
        P("pipe", None, "tensor"),
        P("pipe", None, "tensor"),
        P("pipe", "tensor", None),
        P("pipe", None),
        P("pipe", None),
    )
    return jax.shard_map(
        shards,
        mesh=mesh,
        in_specs=placed,
        out_specs=P(("dp", "pipe", "tensor"), None),
        check_vma=False,
    )
```
